32 devices in a mesh: space: 8 (over z, core), vel: 4 (over y, x).
Axes of the slice: x: 2, y: 2, z: 4, core: 2. Of those that a mesh axis runs over, the one named last changes fastest.
Arguments:
- distribution: float32 [512, 32768], P('space', 'vel'), may hold values from 0.05 to 2
- collision_order: int32 [8, 64], P('space'), may hold values from 0 to 63, each once within a row
- collision_blocks: int32 [8], P('space'), may hold values from 1 to 4, 16 in all
- kernels: float32 [5, 32768], replicated, may hold values from -6 to 6
Outputs:
- new_distribution: float32 [512, 32768], P('space', 'vel')
The draws below stay inside these ranges and needn't reach their ends.
Inputs may be any that keep to these rules, and one draw needn't show every extreme that they name: `collision_order`: each row is an ordering of the 64 local cells. `collision_blocks`: the counts sum to 16, which is 2 on average for each index of space, and the largest is 4.
All inputs are finite; a program needn't handle non-finite values. No bound on the sum of `collision_blocks` on one device may be relied on, other than what follows from the above.
Results may differ from the reference program's by a relative error of at most 0.0001.
Values sent between devices are 32-bit elements; how exact they have to be, the bound alone decides.
A program may use at most 128 MiB of HBM per device.

```python
import math
import jax
import jax.numpy as jnp
import numpy as np
from jax import lax

NV = 32
QUAD = 2
BLOCK_CELLS = 16
CELLS_PER_RANK = 64
MAX_RANK_BLOCKS = 4
KERN = 5
VEL = 32768
CELLS = 512
LISTED_BLOCKS = 16
N_SPACE = 8


def levels(stream_key, dims, cuts, smallest, largest):
    gain = 1.0
    for dim, parts in cuts:
        steps = jax.random.uniform(jax.random.fold_in(jax.random.fold_in(stream_key, 6), dim), (parts,), jnp.float32, smallest / len(cuts), largest / len(cuts))
        gain = gain * jnp.repeat(jnp.exp(steps), dims[dim] // parts).reshape((-1,) + (1,) * (len(dims) - 1 - dim))
    return gain


def profile(amount, total, reach, skew):
    portions = [(1 << 20) // math.isqrt(standing ** skew) + 1 for standing in range(2, amount + 1)]
    spare, holding = total - reach - (amount - 1), [1] * (amount - 1)
    while spare > 0:
        free = [i for i in range(amount - 1) if holding[i] < reach]
        whole, remaining = sum([portions[i] for i in free]), spare
        for i in free:
            addition = min(reach - holding[i], max(1, remaining * portions[i] // whole), spare)
            holding[i] = holding[i] + addition
            spare = spare - addition
    return np.array([reach] + holding)


def uneven_parts(stream_key, number_of, total, limit, skew):
    if number_of == 2:
        one = jax.random.randint(stream_key, (), max(1, total - limit), min(limit, total - 1) + 1)
        return jnp.stack([one, total - one])
    lengths = jnp.asarray(profile(number_of, total, limit, skew), jnp.int32)
    pairs = (number_of - 1) // 2
    source_of, taker = lengths[1:1 + 2 * pairs:2], lengths[2:2 + 2 * pairs:2]
    slack = jnp.minimum(source_of - 1, limit - taker)
    passed = jax.random.randint(jax.random.fold_in(stream_key, 1), (pairs,), 0, 1 << 20) % (slack + 1)
    lengths = lengths.at[1:1 + 2 * pairs:2].set(source_of - passed).at[2:2 + 2 * pairs:2].set(taker + passed)
    return lengths[jax.random.permutation(jax.random.fold_in(stream_key, 2), number_of)]


def bell_draw(rng, dims, width, reach, kind=jnp.bfloat16):
    return jnp.clip(width * jax.random.normal(rng, dims, jnp.float32), -reach, reach).astype(kind)


def setup_inputs(seed: int = 0) -> dict:
    arg_keys = jax.random.split(jax.random.key(seed), 5)
    distribution = jnp.clip(jnp.exp(math.log(2.0) - 3.6888794 * jax.random.uniform(arg_keys[0], (CELLS, VEL), jnp.float32) ** levels(arg_keys[0], (CELLS, VEL), ((0, 8), (1, 4)), -0.2, 0.2)), 0.05, 2.0)
    collision_order = jax.vmap(lambda own: jax.random.permutation(own, CELLS_PER_RANK))(jax.random.split(arg_keys[1], N_SPACE)).reshape((N_SPACE, CELLS_PER_RANK)).astype(jnp.int32)
    collision_blocks = uneven_parts(arg_keys[2], N_SPACE, LISTED_BLOCKS, MAX_RANK_BLOCKS, 2).astype(jnp.int32)
    kernels = bell_draw(arg_keys[3], (KERN, VEL), 1.0, 6.0, jnp.float32)
    return dict(distribution=distribution, collision_order=collision_order, collision_blocks=collision_blocks, kernels=kernels)


STEP_SCALE = 0.25
COURANT_MAX = 0.95


def courants(vel_width):
    vx_plane = (lax.iota(jnp.int32, vel_width) // (NV * NV)).astype(jnp.float32)
    courant = COURANT_MAX * (2.0 * vx_plane - (NV - 1)) / (NV - 1)
    return jnp.maximum(courant, 0.0), jnp.minimum(courant, 0.0)


def sweep(padded, upwind_pos, upwind_neg):
    centre = padded[1:-1]
    return centre - upwind_pos * (centre - padded[:-2]) - upwind_neg * (padded[2:] - centre)


def reference(distribution, collision_order, collision_blocks, kernels):
    upwind_pos, upwind_neg = courants(VEL)
    transported = distribution
    for sweep_turn in range(2):
        transported = sweep(jnp.pad(transported, ((1, 1), (0, 0))), upwind_pos, upwind_neg)
    cell_owner_rank = jnp.argsort(collision_order, axis=1).astype(jnp.int32)
    listed_flag = cell_owner_rank < (BLOCK_CELLS * collision_blocks)[:, None]
    weights = kernels.reshape(KERN, NV, NV, NV)

    def collide(cell_rows):
        velocity_cube = cell_rows.reshape(CELLS_PER_RANK, NV, NV, NV)
        spectrum = jnp.fft.fftn(velocity_cube, axes=(1, 2, 3))

        def inverse(weight):
            return jnp.real(jnp.fft.ifftn(spectrum * weight, axes=(1, 2, 3)))

        gain_term = jnp.zeros_like(velocity_cube)
        for quad_index in range(QUAD):
            gain_term = gain_term + inverse(weights[2 * quad_index]) * inverse(weights[2 * quad_index + 1])
        updated = velocity_cube + STEP_SCALE * (gain_term - velocity_cube * inverse(weights[2 * QUAD]))
        return updated.reshape(CELLS_PER_RANK, VEL)

    grouped = transported.reshape(N_SPACE, CELLS_PER_RANK, VEL)
    collided = lax.map(collide, grouped)
    return jnp.where(listed_flag[:, :, None], collided, grouped).reshape(CELLS, VEL)
```

```python
import functools
import math

import jax
import jax.numpy as jnp
import ml_dtypes
import numpy as np
from jax import lax
from jax.experimental import pallas as pl
from jax.experimental.pallas import tpu as pltpu
from jax.sharding import PartitionSpec as P

NV = 32
QUAD = 2
BLOCK_CELLS = 16
KERN = 5
STEP_SCALE = 0.25
COURANT_MAX = 0.95
LANES = 128
SUB = 8
GROUP = 4
MESH = pl.DeviceIdType.MESH
F32 = jnp.float32
BF16 = jnp.bfloat16


def split_np(matrix):
    high = matrix.astype(ml_dtypes.bfloat16)
    low = (matrix - high.astype(np.float64)).astype(ml_dtypes.bfloat16)
    return high, low


def left_form(matrix):
    real = np.block([[matrix.real, -matrix.imag], [matrix.imag, matrix.real]])
    high, low = split_np(real)
    return np.concatenate([high, low, high], axis=1)


def right_form(matrix):
    real = np.block([[matrix.real, matrix.imag], [-matrix.imag, matrix.real]])
    high, low = split_np(real)
    return np.concatenate([high, high, low], axis=0)


def dft_constants():
    turn = lambda phase: np.exp(-2j * math.pi * phase)
    r = np.repeat(np.arange(8), 16)[:, None]
    p = np.tile(np.arange(16), 8)[:, None]
    x0 = np.repeat(np.arange(16), 8)[None, :]
    y1 = np.tile(np.arange(8), 16)[None, :]
    y0 = np.repeat(np.arange(4), 32)[:, None]
    z = np.tile(np.arange(32), 4)[:, None]
    s, qz = y0.T, z.T
    rows = [turn(y1 * r / 8 + x0 * p / 16 + x0 * h / 32) for h in range(2)]
    lanes = turn(y0 * s / 4 + z * qz / 32)
    twist = turn(r * y0.T / 32)
    return (
        np.stack([left_form(m) for m in rows]),
        right_form(lanes),
        np.stack([left_form(m.conj().T) for m in rows]),
        right_form(lanes.conj().T),
        np.stack([twist.real, twist.imag]).astype(np.float32),
    )


def halves(value):
    high = value.astype(BF16)
    return high, (value - high.astype(F32)).astype(BF16)


def left_dot(table, value):
    high, low = halves(value)
    return jnp.dot(table, jnp.concatenate([high, high, low], axis=0), preferred_element_type=F32)


def right_dot(value, table):
    high, low = halves(value)
    return jnp.dot(jnp.concatenate([high, low, high], axis=1), table, preferred_element_type=F32)


def kernel(
    n_space, n_vel, cells, width,
    dist_ref, listed_ref, weight_ref, fr_ref, fl_ref, br_ref, bl_ref, tw_ref,
    out_ref,
    padded, halo_out, halo_in, sent, got, result, back, spectrum, parts,
    in_sem, halo_send, halo_recv, fs_sem, fr_sem, bs_sem, br_sem, own_sem,
):
    rows = width // LANES
    own = cells // n_vel
    groups = own // GROUP
    piece = GROUP * rows
    pairs = GROUP // 2
    me = lax.axis_index("vel")
    spot = lax.axis_index("space")
    right, left = lax.rem(spot + 1, n_space), lax.rem(spot + n_space - 1, n_space)

    load = pltpu.make_async_copy(dist_ref, padded.at[pl.ds(SUB, cells)], in_sem)
    load.start()
    barrier = pltpu.get_barrier_semaphore()
    for step in range(1, n_vel):
        pl.semaphore_signal(
            barrier, inc=1, device_id={"vel": lax.rem(me + step, n_vel)}, device_id_type=MESH
        )
    for side in (left, right):
        pl.semaphore_signal(barrier, inc=1, device_id={"space": side}, device_id_type=MESH)
    load.wait()

    @pl.loop(0, rows)
    def _(k):
        lanes = pl.ds(pl.multiple_of(k * LANES, LANES), LANES)
        halo_out[0, pl.ds(2 * k, 2), :] = padded[SUB:SUB + 2, lanes]
        halo_out[1, pl.ds(2 * k, 2), :] = padded[SUB + cells - 2:SUB + cells, lanes]

    pl.semaphore_wait(barrier, n_vel + 1)
    halo_copies = []
    for way, side in ((0, left), (1, right)):
        copy = pltpu.make_async_remote_copy(
            src_ref=halo_out.at[way],
            dst_ref=halo_in.at[1 - way],
            send_sem=halo_send.at[way],
            recv_sem=halo_recv.at[1 - way],
            device_id={"space": side},
            device_id_type=MESH,
        )
        copy.start()
        halo_copies.append(copy)
    for copy in halo_copies:
        copy.wait()

    total = cells + 2 * SUB
    position = lax.broadcasted_iota(jnp.int32, (total, LANES), 0) + (spot * cells - SUB)
    inside = (position >= 0) & (position < n_space * cells)

    @pl.loop(0, rows)
    def _(k):
        lanes = pl.ds(pl.multiple_of(k * LANES, LANES), LANES)
        padded[SUB - 2:SUB, lanes] = halo_in[0, pl.ds(2 * k, 2), :]
        padded[SUB + cells:SUB + cells + 2, lanes] = halo_in[1, pl.ds(2 * k, 2), :]
        plane = (me * rows + k) // SUB
        courant = COURANT_MAX * (2.0 * plane.astype(F32) - (NV - 1)) / (NV - 1)
        upwind_pos, upwind_neg = jnp.maximum(courant, 0.0), jnp.minimum(courant, 0.0)
        value = jnp.where(inside, padded[:, lanes], 0.0)
        for _ in range(2):
            before = pltpu.roll(value, 1, 0)
            after = pltpu.roll(value, total - 1, 0)
            value = value - upwind_pos * (value - before) - upwind_neg * (after - value)
            value = jnp.where(inside, value, 0.0)
        for tile in range(cells // SUB):
            sent[pl.ds(tile * SUB * rows + k, SUB, stride=rows), :] = value[
                (tile + 1) * SUB:(tile + 2) * SUB
            ]

    def forward(group, step):
        target = lax.rem(me + step, n_vel)
        return pltpu.make_async_remote_copy(
            src_ref=sent.at[pl.ds((target * groups + group) * piece, piece)],
            dst_ref=got.at[group, me],
            send_sem=fs_sem.at[group, step],
            recv_sem=fr_sem.at[group, step],
            device_id={"vel": target},
            device_id_type=MESH,
        )

    def backward(group, step):
        target = lax.rem(me + step, n_vel)
        return pltpu.make_async_remote_copy(
            src_ref=result.at[group, target],
            dst_ref=back.at[pl.ds((me * groups + group) * piece, piece)],
            send_sem=bs_sem.at[group, step],
            recv_sem=br_sem.at[group, step],
            device_id={"vel": target},
            device_id_type=MESH,
        )

    def own_in(group):
        return pltpu.make_async_copy(
            sent.at[pl.ds((me * groups + group) * piece, piece)], got.at[group, me],
            own_sem.at[0, group],
        )

    def own_out(group):
        return pltpu.make_async_copy(
            result.at[group, me], back.at[pl.ds((me * groups + group) * piece, piece)],
            own_sem.at[1, group],
        )

    for group in range(groups):
        for step in range(1, n_vel):
            forward(group, step).start()
        own_in(group).start()

    half = NV * SUB // 2

    @pl.loop(0, groups)
    def _(group):
        for step in range(1, n_vel):
            forward(group, step).wait_recv()
        own_in(group).wait()

        def cell(j):
            return jnp.concatenate(
                [got[group, m, j * rows:(j + 1) * rows, :] for m in range(n_vel)], axis=0
            )

        def stacked(lower):
            cut = slice(0, half) if lower else slice(half, 2 * half)
            return jnp.concatenate(
                [
                    jnp.concatenate([cell(2 * i)[cut], cell(2 * i + 1)[cut]], axis=0)
                    for i in range(pairs)
                ],
                axis=1,
            )

        twist_re, twist_im = tw_ref[0], tw_ref[1]
        low, high = stacked(True), stacked(False)
        for h, mixed in enumerate((low + high, low - high)):
            turned = left_dot(fr_ref[h], mixed)
            for i in range(pairs):
                re = turned[:half, i * LANES:(i + 1) * LANES]
                im = turned[half:, i * LANES:(i + 1) * LANES]
                spectrum[(2 * i + h) * half:(2 * i + h + 1) * half, :] = jnp.concatenate(
                    [re * twist_re - im * twist_im, re * twist_im + im * twist_re], axis=1
                )
        spectrum[...] = right_dot(spectrum[...], fl_ref[...])

        for table in range(KERN):
            weight = weight_ref[table]
            weights = jnp.concatenate([weight] * pairs, axis=0)
            weights = jnp.concatenate([weights, weights], axis=1)
            lined = right_dot(spectrum[...] * weights, bl_ref[...])
            halves_out = []
            for h in range(2):
                columns = []
                for i in range(pairs):
                    block = lined[(2 * i + h) * half:(2 * i + h + 1) * half]
                    re, im = block[:, :LANES], block[:, LANES:]
                    columns.append(
                        jnp.concatenate(
                            [re * twist_re + im * twist_im, im * twist_re - re * twist_im], axis=0
                        )
                    )
                halves_out.append(left_dot(br_ref[h], jnp.concatenate(columns, axis=1)))
            even, odd = halves_out
            for place, value in ((0, even + odd), (1, even - odd)):
                if table == 0:
                    parts[place] = value
                elif table == 1:
                    parts[place] = parts[place] * value
                elif table == 2:
                    parts[2 + place] = value
                elif table == 3:
                    parts[place] = parts[place] + parts[2 + place] * value
                else:
                    parts[place] = parts[place] - stacked(place == 0) * value

        for j in range(GROUP):
            flag = listed_ref[pl.ds((me * groups + group) * GROUP + j, 1), :] > 0.0
            i, component = j // 2, j % 2
            for m in range(n_vel):
                place, start = (m * rows) // half, (m * rows) % half
                change = parts[
                    place,
                    component * half + start:component * half + start + rows,
                    i * LANES:(i + 1) * LANES,
                ]
                old = got[group, m, j * rows:(j + 1) * rows, :]
                result[group, m, j * rows:(j + 1) * rows, :] = jnp.where(
                    flag, old + STEP_SCALE * change, old
                )
        for step in range(1, n_vel):
            backward(group, step).start()
        own_out(group).start()

    for group in range(groups):
        for step in range(1, n_vel):
            forward(group, step).wait_send()
            backward(group, step).wait()
        own_out(group).wait()

    @pl.loop(0, rows)
    def _(k):
        lanes = pl.ds(pl.multiple_of(k * LANES, LANES), LANES)
        for tile in range(cells // SUB):
            out_ref[tile * SUB:(tile + 1) * SUB, lanes] = back[
                pl.ds(tile * SUB * rows + k, SUB, stride=rows), :
            ]


def packed_weights(kernels):
    cube = kernels.reshape(KERN, NV, NV, NV)
    mirrored = jnp.roll(jnp.flip(cube, (1, 2, 3)), (1, 1, 1), (1, 2, 3))
    even = (cube + mirrored) * (0.5 / NV**3)
    even = even.reshape(KERN, NV // 2, 2, 4, 8, NV).transpose(0, 2, 4, 1, 3, 5)
    return even.reshape(KERN, NV * SUB, LANES)


def local(n_space, n_vel, distribution, collision_order, collision_blocks, kernels):
    cells, width = distribution.shape
    rows = width // LANES
    own = cells // n_vel
    groups = own // GROUP
    piece = GROUP * rows
    slot = lax.iota(jnp.int32, cells)
    chosen = (slot < BLOCK_CELLS * collision_blocks[0])[:, None]
    hit = (collision_order[0][:, None] == slot[None, :]) & chosen
    listed = jnp.broadcast_to(jnp.max(hit.astype(F32), axis=0)[:, None], (cells, LANES))
    weights = packed_weights(kernels)
    constants = [jnp.asarray(c) for c in dft_constants()]
    vmem = pl.BlockSpec(memory_space=pltpu.VMEM)
    dma = pltpu.SemaphoreType.DMA
    return pl.pallas_call(
        functools.partial(kernel, n_space, n_vel, cells, width),
        out_shape=jax.ShapeDtypeStruct((cells, width), F32),
        in_specs=[pl.BlockSpec(memory_space=pl.ANY)] + [vmem] * 7,
        out_specs=vmem,
        scratch_shapes=[
            pltpu.VMEM((cells + 2 * SUB, width), F32),
            pltpu.VMEM((2, 2 * rows, LANES), F32),
            pltpu.VMEM((2, 2 * rows, LANES), F32),
            pltpu.VMEM((cells * rows, LANES), F32),
            pltpu.VMEM((groups, n_vel, piece, LANES), F32),
            pltpu.VMEM((groups, n_vel, piece, LANES), F32),
            pltpu.VMEM((cells * rows, LANES), F32),
            pltpu.VMEM((GROUP // 2 * NV * SUB, 2 * LANES), F32),
            pltpu.VMEM((4, NV * SUB, GROUP // 2 * LANES), F32),
            dma,
            dma((2,)),
            dma((2,)),
            dma((groups, n_vel)),
            dma((groups, n_vel)),
            dma((groups, n_vel)),
            dma((groups, n_vel)),
            dma((2, groups)),
        ],
        compiler_params=pltpu.CompilerParams(
            collective_id=0, has_side_effects=True, vmem_limit_bytes=48 * 2**20
        ),
    )(distribution, listed, weights, *constants)


def solution(mesh):
    return jax.shard_map(
        functools.partial(local, mesh.shape["space"], mesh.shape["vel"]),
        mesh=mesh,
        in_specs=(P("space", "vel"), P("space", None), P("space"), P()),
        out_specs=P("space", "vel"),
        check_vma=False,
    )
```

```python
import functools
import math

import jax
import jax.numpy as jnp
import numpy as np
from jax import lax
from jax.experimental import pallas as pl
from jax.experimental.pallas import tpu as pltpu
from jax.sharding import PartitionSpec as P

NV = 32
QUAD = 2
BLOCK_CELLS = 16
KERN = 5
STEP_SCALE = 0.25
COURANT_MAX = 0.95
LANES = 128
SUB = 8
GROUP = 4
MESH = pl.DeviceIdType.MESH
F32 = jnp.float32
BF16 = jnp.bfloat16


def left_form(matrix):
    return np.block([[matrix.real, -matrix.imag], [matrix.imag, matrix.real]])


def right_form(matrix):
    return np.block([[matrix.real, matrix.imag], [-matrix.imag, matrix.real]])


def dft_constants():
    turn = lambda phase: np.exp(-2j * math.pi * phase)
    r = np.repeat(np.arange(8), 16)[:, None]
    p = np.tile(np.arange(16), 8)[:, None]
    x0 = np.repeat(np.arange(16), 8)[None, :]
    y1 = np.tile(np.arange(8), 16)[None, :]
    y0 = np.repeat(np.arange(4), 32)[:, None]
    z = np.tile(np.arange(32), 4)[:, None]
    s, qz = y0.T, z.T
    rows = [turn(y1 * r / 8 + x0 * p / 16 + x0 * h / 32) for h in range(2)]
    lanes = turn(y0 * s / 4 + z * qz / 32)
    twist = turn(r * y0.T / 32)
    steps = [left_form(m) for m in rows] + [left_form(m.conj().T) for m in rows]
    steps += [right_form(lanes), right_form(lanes.conj().T)]
    return (
        np.stack(steps).astype(np.float32),
        np.stack([twist.real, twist.imag]).astype(np.float32),
        mirrors().astype(np.float32),
    )


def mirrors():
    lane = np.arange(LANES)
    s, qz = lane // NV, lane % NV
    moves = []
    for carry in range(2):
        source = (-s - carry) % 4 * NV + -qz % NV
        moves.append((lane[:, None] == source[None, :]).astype(np.float64))
    row = np.arange(NV * SUB)
    h, r, p = row // LANES, row // 16 % 8, row % 16
    source = h * LANES + -r % 8 * 16 + (-p - h) % 16
    rows = (source[:, None] == row[None, :]).astype(np.float64)
    return np.concatenate([np.concatenate(moves, axis=1), rows])


def halves(value):
    high = value.astype(BF16)
    return high, (value - high.astype(F32)).astype(BF16)


def left_dot(table, value):
    high, low = halves(value)
    return jnp.dot(table, jnp.concatenate([high, high, low], axis=0), preferred_element_type=F32)


def right_dot(value, table):
    high, low = halves(value)
    return jnp.dot(jnp.concatenate([high, low, high], axis=1), table, preferred_element_type=F32)


def kernel(
    n_space, n_vel, cells, width,
    dist_ref, order_ref, blocks_ref, kernels_ref, *refs,
):
    tables_hbm, out_ref, refs = refs[:3], refs[3], refs[4:]
    tables, refs = refs[:3], refs[3:]
    step_ref, tw_ref, mirror_ref = tables
    (padded, halo_out, halo_in, sent, got, result, back, spectrum, parts,
    left_ref, right_ref, raw, natural, weight_ref, staged, listed_ref, raw_sem, in_sem, table_sem, out_sem,
    halo_send, halo_recv, fs_sem, fr_sem, bs_sem, br_sem, own_sem) = refs
    rows = width // LANES
    own = cells // n_vel
    groups = own // GROUP
    piece = GROUP * rows
    pairs = GROUP // 2
    me = lax.axis_index("vel")
    spot = lax.axis_index("space")
    right, left = lax.rem(spot + 1, n_space), lax.rem(spot + n_space - 1, n_space)

    load = pltpu.make_async_copy(dist_ref, padded.at[pl.ds(SUB, cells)], in_sem)
    load.start()
    load_raw = pltpu.make_async_copy(kernels_ref, raw, raw_sem)
    load_raw.start()
    load_tables = [
        pltpu.make_async_copy(source, table, table_sem.at[i])
        for i, (source, table) in enumerate(zip(tables_hbm, tables))
    ]
    for copy in load_tables:
        copy.start()
    barrier = pltpu.get_barrier_semaphore()
    for step in range(1, n_vel):
        pl.semaphore_signal(
            barrier, inc=1, device_id={"vel": lax.rem(me + step, n_vel)}, device_id_type=MESH
        )
    for side in (left, right):
        pl.semaphore_signal(barrier, inc=1, device_id={"space": side}, device_id_type=MESH)
    load.wait()

    @pl.loop(0, rows)
    def _(k):
        lanes = pl.ds(pl.multiple_of(k * LANES, LANES), LANES)
        halo_out[0, pl.ds(2 * k, 2), :] = padded[SUB:SUB + 2, lanes]
        halo_out[1, pl.ds(2 * k, 2), :] = padded[SUB + cells - 2:SUB + cells, lanes]

    pl.semaphore_wait(barrier, n_vel + 1)
    halo_copies = []
    for way, side in ((0, left), (1, right)):
        copy = pltpu.make_async_remote_copy(
            src_ref=halo_out.at[way],
            dst_ref=halo_in.at[1 - way],
            send_sem=halo_send.at[way],
            recv_sem=halo_recv.at[1 - way],
            device_id={"space": side},
            device_id_type=MESH,
        )
        copy.start()
        halo_copies.append(copy)

    def swept(value, k, inside=None):
        plane = (me * rows + k) // SUB
        courant = COURANT_MAX * (2.0 * plane.astype(F32) - (NV - 1)) / (NV - 1)
        upwind_pos, upwind_neg = jnp.maximum(courant, 0.0), jnp.minimum(courant, 0.0)
        extent = value.shape[0]
        for _ in range(2):
            before = pltpu.roll(value, 1, 0)
            after = pltpu.roll(value, extent - 1, 0)
            value = value - upwind_pos * (value - before) - upwind_neg * (after - value)
            if inside is not None:
                value = jnp.where(inside, value, 0.0)
        return value

    @pl.loop(0, rows)
    def _(k):
        lanes = pl.ds(pl.multiple_of(k * LANES, LANES), LANES)
        value = swept(padded[SUB:SUB + cells, lanes], k)
        for tile in range(cells // SUB):
            sent[pl.ds(tile * SUB * rows + k, SUB, stride=rows), :] = value[
                tile * SUB:(tile + 1) * SUB
            ]

    def forward(group, step):
        target = lax.rem(me + step, n_vel)
        return pltpu.make_async_remote_copy(
            src_ref=sent.at[pl.ds((target * groups + group) * piece, piece)],
            dst_ref=got.at[group, me],
            send_sem=fs_sem.at[group, step],
            recv_sem=fr_sem.at[group, step],
            device_id={"vel": target},
            device_id_type=MESH,
        )

    def backward(group, step):
        target = lax.rem(me + step, n_vel)
        return pltpu.make_async_remote_copy(
            src_ref=result.at[group, target],
            dst_ref=back.at[pl.ds((me * groups + group) * piece, piece)],
            send_sem=bs_sem.at[group, step],
            recv_sem=br_sem.at[group, step],
            device_id={"vel": target},
            device_id_type=MESH,
        )

    def own_in(group):
        return pltpu.make_async_copy(
            sent.at[pl.ds((me * groups + group) * piece, piece)], got.at[group, me],
            own_sem.at[0, group],
        )

    def own_out(group):
        return pltpu.make_async_copy(
            result.at[group, me], back.at[pl.ds((me * groups + group) * piece, piece)],
            own_sem.at[1, group],
        )

    def send(group):
        for step in range(1, n_vel):
            forward(group, step).start()
        own_in(group).start()

    inner = [group for group in range(groups) if 0 < group < groups - 1]
    outer = [group for group in range(groups) if group not in inner]
    for group in inner:
        send(group)
    for copy in halo_copies:
        copy.wait()

    edge = 2 * SUB
    for side in range(2):
        base = 0 if side == 0 else cells
        position = lax.broadcasted_iota(jnp.int32, (edge, LANES), 0) + (spot * cells + base - SUB)
        inside = (position >= 0) & (position < n_space * cells)

        @pl.loop(0, rows)
        def _(k):
            lanes = pl.ds(pl.multiple_of(k * LANES, LANES), LANES)
            if side == 0:
                padded[SUB - 2:SUB, lanes] = halo_in[0, pl.ds(2 * k, 2), :]
            else:
                padded[SUB + cells:SUB + cells + 2, lanes] = halo_in[1, pl.ds(2 * k, 2), :]
            value = jnp.where(inside, padded[base:base + edge, lanes], 0.0)
            value = swept(value, k, inside)
            if side == 0:
                sent[pl.ds(k, 2, stride=rows), :] = value[SUB:SUB + 2]
            else:
                sent[pl.ds((cells - 2) * rows + k, 2, stride=rows), :] = value[SUB - 2:SUB]

    for group in outer:
        send(group)

    slot = lax.broadcasted_iota(jnp.int32, (cells, cells), 1)
    cell_id = lax.broadcasted_iota(jnp.int32, (cells, cells), 0)
    chosen = slot < BLOCK_CELLS * jnp.broadcast_to(blocks_ref[...], (cells, cells))
    hit = (jnp.broadcast_to(order_ref[...], (cells, cells)) == cell_id) & chosen
    flags = jnp.max(jnp.where(hit, 1.0, 0.0), axis=1, keepdims=True)
    listed_ref[...] = jnp.broadcast_to(flags, (cells, LANES))

    load_raw.wait()
    for copy in load_tables:
        copy.wait()
    for i in range(4):
        high, low = halves(step_ref[i])
        left_ref[i] = jnp.concatenate([high, low, high], axis=1)
    for i in range(2):
        high, low = halves(step_ref[4 + i])
        right_ref[i] = jnp.concatenate([high, high, low], axis=0)
    for k in range(NV * SUB):
        natural[pl.ds(k, KERN, stride=NV * SUB), :] = raw[:, k * LANES:(k + 1) * LANES]
    lane_block = lax.broadcasted_iota(jnp.int32, (SUB, LANES), 1) // NV
    row_r = lax.broadcasted_iota(jnp.int32, (NV * SUB, LANES), 0) // 16 % 8

    @pl.loop(0, KERN)
    def _(table):
        base = table * (NV * SUB)
        for h in range(2):
            for r in range(8):
                for p in (0, 8):
                    packed = None
                    for s in range(4):
                        start = (2 * p + h) * SUB + 2 * s + r // 4
                        block = natural[pl.ds(base + start, SUB, stride=2 * SUB), :]
                        shift = (s - r % 4) % 4 * NV
                        if shift:
                            block = pltpu.roll(block, shift, 1)
                        packed = block if s == 0 else jnp.where(lane_block == s, block, packed)
                    top = h * LANES + r * 16 + p
                    staged[top:top + SUB, :] = packed
        value = staged[...]
        high, low = halves(value)
        lane_moves, row_moves = mirror_ref[:LANES].astype(BF16), mirror_ref[LANES:].astype(BF16)
        moved = jnp.dot(high, lane_moves, preferred_element_type=F32) + jnp.dot(
            low, lane_moves, preferred_element_type=F32
        )
        moved = jnp.where(row_r == 0, moved[:, :LANES], moved[:, LANES:])
        high, low = halves(moved)
        moved = jnp.dot(
            row_moves, jnp.concatenate([high, low], axis=1), preferred_element_type=F32
        )
        moved = moved[:, :LANES] + moved[:, LANES:]
        weight_ref[table] = (value + moved) * (0.5 / NV**3)

    half = NV * SUB // 2

    def work(group):
        def cell(j):
            return jnp.concatenate(
                [got[group, m, j * rows:(j + 1) * rows, :] for m in range(n_vel)], axis=0
            )

        def stacked(lower):
            cut = slice(0, half) if lower else slice(half, 2 * half)
            return jnp.concatenate(
                [
                    jnp.concatenate([cell(2 * i)[cut], cell(2 * i + 1)[cut]], axis=0)
                    for i in range(pairs)
                ],
                axis=1,
            )

        twist_re, twist_im = tw_ref[0], tw_ref[1]
        low, high = stacked(True), stacked(False)
        for h, mixed in enumerate((low + high, low - high)):
            turned = left_dot(left_ref[h], mixed)
            for i in range(pairs):
                re = turned[:half, i * LANES:(i + 1) * LANES]
                im = turned[half:, i * LANES:(i + 1) * LANES]
                spectrum[(2 * i + h) * half:(2 * i + h + 1) * half, :] = jnp.concatenate(
                    [re * twist_re - im * twist_im, re * twist_im + im * twist_re], axis=1
                )
        spectrum[...] = right_dot(spectrum[...], right_ref[0])

        for table in range(KERN):
            weight = weight_ref[table]
            weights = jnp.concatenate([weight] * pairs, axis=0)
            weights = jnp.concatenate([weights, weights], axis=1)
            lined = right_dot(spectrum[...] * weights, right_ref[1])
            halves_out = []
            for h in range(2):
                columns = []
                for i in range(pairs):
                    block = lined[(2 * i + h) * half:(2 * i + h + 1) * half]
                    re, im = block[:, :LANES], block[:, LANES:]
                    columns.append(
                        jnp.concatenate(
                            [re * twist_re + im * twist_im, im * twist_re - re * twist_im], axis=0
                        )
                    )
                halves_out.append(left_dot(left_ref[2 + h], jnp.concatenate(columns, axis=1)))
            even, odd = halves_out
            for place, value in ((0, even + odd), (1, even - odd)):
                if table == 0:
                    parts[place] = value
                elif table == 1:
                    parts[place] = parts[place] * value
                elif table == 2:
                    parts[2 + place] = value
                elif table == 3:
                    parts[place] = parts[place] + parts[2 + place] * value
                else:
                    parts[place] = parts[place] - stacked(place == 0) * value

        for j in range(GROUP):
            flag = listed_ref[pl.ds((me * groups + group) * GROUP + j, 1), :] > 0.0
            i, component = j // 2, j % 2
            for m in range(n_vel):
                place, start = (m * rows) // half, (m * rows) % half
                change = parts[
                    place,
                    component * half + start:component * half + start + rows,
                    i * LANES:(i + 1) * LANES,
                ]
                old = got[group, m, j * rows:(j + 1) * rows, :]
                result[group, m, j * rows:(j + 1) * rows, :] = jnp.where(
                    flag, old + STEP_SCALE * change, old
                )

    def give(group):
        for step in range(1, n_vel):
            backward(group, step).start()
        own_out(group).start()

    turns = inner + outer
    count = len(inner)

    def group_of(turn):
        if groups == 1:
            return turn
        return jnp.where(turn < count, turn + 1, (turn - count) * (groups - 1))

    @pl.loop(0, groups)
    def _(turn):
        group = group_of(turn)
        for step in range(1, n_vel):
            forward(group, step).wait_recv()
        own_in(group).wait()
        if groups > 2:
            @pl.when(turn == groups - 1)
            def _():
                give(group_of(turn - 1))

        work(group)

        if groups > 2:
            @pl.when((turn > 0) & (turn < groups - 1))
            def _():
                give(group_of(turn - 1))

            @pl.when(turn == groups - 1)
            def _():
                give(group)
        else:
            give(group)

    for group in range(groups):
        for step in range(1, n_vel):
            forward(group, step).wait_send()

    def finish(tiles):
        @pl.loop(0, rows)
        def _(k):
            lanes = pl.ds(pl.multiple_of(k * LANES, LANES), LANES)
            for tile in tiles:
                padded[tile * SUB:(tile + 1) * SUB, lanes] = back[
                    pl.ds(tile * SUB * rows + k, SUB, stride=rows), :
                ]

        copies = []
        for tile in tiles:
            part = pl.ds(tile * SUB, SUB)
            copies.append(pltpu.make_async_copy(padded.at[part], out_ref.at[part], out_sem.at[tile]))
            copies[-1].start()
        return copies

    done, ready, copies = set(), set(), []
    for group in turns:
        for step in range(1, n_vel):
            backward(group, step).wait()
        own_out(group).wait()
        ready.add(group)
        tiles = []
        for tile in range(cells // SUB):
            needs = {cell % own // GROUP for cell in range(tile * SUB, (tile + 1) * SUB)}
            if tile not in done and needs <= ready:
                tiles.append(tile)
        done.update(tiles)
        if tiles:
            copies += finish(tiles)
    for copy in copies:
        copy.wait()


def local(n_space, n_vel, distribution, collision_order, collision_blocks, kernels):
    cells, width = distribution.shape
    rows = width // LANES
    own = cells // n_vel
    groups = own // GROUP
    piece = GROUP * rows
    constants = [jnp.asarray(c) for c in dft_constants()]
    anywhere = pl.BlockSpec(memory_space=pl.ANY)
    vmem = pl.BlockSpec(memory_space=pltpu.VMEM)
    dma = pltpu.SemaphoreType.DMA
    return pl.pallas_call(
        functools.partial(kernel, n_space, n_vel, cells, width),
        out_shape=jax.ShapeDtypeStruct((cells, width), F32),
        in_specs=[anywhere, vmem, vmem] + [anywhere] * 4,
        out_specs=anywhere,
        scratch_shapes=[pltpu.VMEM(c.shape, c.dtype) for c in constants]
        + [
            pltpu.VMEM((cells + 2 * SUB, width), F32),
            pltpu.VMEM((2, 2 * rows, LANES), F32),
            pltpu.VMEM((2, 2 * rows, LANES), F32),
            pltpu.VMEM((cells * rows, LANES), F32),
            pltpu.VMEM((groups, n_vel, piece, LANES), F32),
            pltpu.VMEM((groups, n_vel, piece, LANES), F32),
            pltpu.VMEM((cells * rows, LANES), F32),
            pltpu.VMEM((GROUP // 2 * NV * SUB, 2 * LANES), F32),
            pltpu.VMEM((4, NV * SUB, GROUP // 2 * LANES), F32),
            pltpu.VMEM((4, NV * SUB, 3 * NV * SUB), BF16),
            pltpu.VMEM((2, 3 * NV * SUB, NV * SUB), BF16),
            pltpu.VMEM((KERN, NV**3), F32),
            pltpu.VMEM((KERN * NV * SUB, LANES), F32),
            pltpu.VMEM((KERN, NV * SUB, LANES), F32),
            pltpu.VMEM((NV * SUB, LANES), F32),
            pltpu.VMEM((cells, LANES), F32),
            dma,
            dma,
            dma((len(constants),)),
            dma((cells // SUB,)),
            dma((2,)),
            dma((2,)),
            dma((groups, n_vel)),
            dma((groups, n_vel)),
            dma((groups, n_vel)),
            dma((groups, n_vel)),
            dma((2, groups)),
        ],
        compiler_params=pltpu.CompilerParams(
            collective_id=0, has_side_effects=True, vmem_limit_bytes=60 * 2**20
        ),
    )(distribution, collision_order, collision_blocks[:, None], kernels, *constants)


def solution(mesh):
    return jax.shard_map(
        functools.partial(local, mesh.shape["space"], mesh.shape["vel"]),
        mesh=mesh,
        in_specs=(P("space", "vel"), P("space", None), P("space"), P()),
        out_specs=P("space", "vel"),
        check_vma=False,
    )
```

```python
import functools
import math

import jax
import jax.numpy as jnp
import numpy as np
from jax import lax
from jax.experimental import pallas as pl
from jax.experimental.pallas import tpu as pltpu
from jax.sharding import PartitionSpec as P

NV = 32
QUAD = 2
BLOCK_CELLS = 16
KERN = 5
STEP_SCALE = 0.25
COURANT_MAX = 0.95
LANES = 128
SUB = 8
GROUP = 4
MESH = pl.DeviceIdType.MESH
F32 = jnp.float32
BF16 = jnp.bfloat16


def left_form(matrix):
    return np.block([[matrix.real, -matrix.imag], [matrix.imag, matrix.real]])


def right_form(matrix):
    return np.block([[matrix.real, matrix.imag], [-matrix.imag, matrix.real]])


def dft_constants():
    turn = lambda phase: np.exp(-2j * math.pi * phase)
    r = np.repeat(np.arange(8), 16)[:, None]
    p = np.tile(np.arange(16), 8)[:, None]
    x0 = np.repeat(np.arange(16), 8)[None, :]
    y1 = np.tile(np.arange(8), 16)[None, :]
    y0 = np.repeat(np.arange(4), 32)[:, None]
    z = np.tile(np.arange(32), 4)[:, None]
    s, qz = y0.T, z.T
    rows = [turn(y1 * r / 8 + x0 * p / 16 + x0 * h / 32) for h in range(2)]
    lanes = turn(y0 * s / 4 + z * qz / 32)
    twist = turn(r * y0.T / 32)
    steps = [left_form(m) for m in rows] + [left_form(m.conj().T) for m in rows]
    steps += [right_form(lanes), right_form(lanes.conj().T)]
    return (
        np.stack(steps).astype(np.float32),
        np.stack([twist.real, twist.imag]).astype(np.float32),
        mirrors().astype(np.float32),
    )


def mirrors():
    lane = np.arange(LANES)
    s, qz = lane // NV, lane % NV
    moves = []
    for carry in range(2):
        source = (-s - carry) % 4 * NV + -qz % NV
        moves.append((lane[:, None] == source[None, :]).astype(np.float64))
    row = np.arange(NV * SUB)
    h, r, p = row // LANES, row // 16 % 8, row % 16
    source = h * LANES + -r % 8 * 16 + (-p - h) % 16
    rows = (source[:, None] == row[None, :]).astype(np.float64)
    return np.concatenate([np.concatenate(moves, axis=1), rows])


def halves(value):
    high = value.astype(BF16)
    return high, (value - high.astype(F32)).astype(BF16)


def left_dot(table, value):
    high, low = halves(value)
    return jnp.dot(table, jnp.concatenate([high, high, low], axis=0), preferred_element_type=F32)


def right_dot(value, table):
    high, low = halves(value)
    return jnp.dot(jnp.concatenate([high, low, high], axis=1), table, preferred_element_type=F32)


def kernel(
    n_space, n_vel, cells, width,
    dist_ref, order_ref, blocks_ref, kernels_ref, *refs,
):
    tables_hbm, out_ref, refs = refs[:3], refs[3], refs[4:]
    tables, refs = refs[:3], refs[3:]
    step_ref, tw_ref, mirror_ref = tables
    (padded, halo_out, halo_in, sent, got, result, back, spectrum, parts,
    left_ref, right_ref, raw, natural, weight_ref, staged, listed_ref, raw_sem, in_sem, table_sem,
    halo_send, halo_recv, fs_sem, fr_sem, bs_sem, br_sem, own_sem) = refs
    rows = width // LANES
    own = cells // n_vel
    groups = own // GROUP
    piece = GROUP * rows
    pairs = GROUP // 2
    me = lax.axis_index("vel")
    spot = lax.axis_index("space")
    right, left = lax.rem(spot + 1, n_space), lax.rem(spot + n_space - 1, n_space)

    load = pltpu.make_async_copy(dist_ref, padded.at[pl.ds(SUB, cells)], in_sem)
    load.start()
    load_raw = pltpu.make_async_copy(kernels_ref, raw, raw_sem)
    load_raw.start()
    load_tables = [
        pltpu.make_async_copy(source, table, table_sem.at[i])
        for i, (source, table) in enumerate(zip(tables_hbm, tables))
    ]
    for copy in load_tables:
        copy.start()
    barrier = pltpu.get_barrier_semaphore()
    for step in range(1, n_vel):
        pl.semaphore_signal(
            barrier, inc=1, device_id={"vel": lax.rem(me + step, n_vel)}, device_id_type=MESH
        )
    for side in (left, right):
        pl.semaphore_signal(barrier, inc=1, device_id={"space": side}, device_id_type=MESH)
    load.wait()

    @pl.loop(0, rows)
    def _(k):
        lanes = pl.ds(pl.multiple_of(k * LANES, LANES), LANES)
        halo_out[0, pl.ds(2 * k, 2), :] = padded[SUB:SUB + 2, lanes]
        halo_out[1, pl.ds(2 * k, 2), :] = padded[SUB + cells - 2:SUB + cells, lanes]

    pl.semaphore_wait(barrier, n_vel + 1)
    halo_copies = []
    for way, side in ((0, left), (1, right)):
        copy = pltpu.make_async_remote_copy(
            src_ref=halo_out.at[way],
            dst_ref=halo_in.at[1 - way],
            send_sem=halo_send.at[way],
            recv_sem=halo_recv.at[1 - way],
            device_id={"space": side},
            device_id_type=MESH,
        )
        copy.start()
        halo_copies.append(copy)

    def swept(value, k, inside=None):
        plane = (me * rows + k) // SUB
        courant = COURANT_MAX * (2.0 * plane.astype(F32) - (NV - 1)) / (NV - 1)
        upwind_pos, upwind_neg = jnp.maximum(courant, 0.0), jnp.minimum(courant, 0.0)
        extent = value.shape[0]
        for _ in range(2):
            before = pltpu.roll(value, 1, 0)
            after = pltpu.roll(value, extent - 1, 0)
            value = value - upwind_pos * (value - before) - upwind_neg * (after - value)
            if inside is not None:
                value = jnp.where(inside, value, 0.0)
        return value

    def forward(group, step):
        target = lax.rem(me + step, n_vel)
        return pltpu.make_async_remote_copy(
            src_ref=sent.at[pl.ds((target * groups + group) * piece, piece)],
            dst_ref=got.at[group, me],
            send_sem=fs_sem.at[group, step],
            recv_sem=fr_sem.at[group, step],
            device_id={"vel": target},
            device_id_type=MESH,
        )

    def backward(group, step):
        target = lax.rem(me + step, n_vel)
        return pltpu.make_async_remote_copy(
            src_ref=result.at[group, target],
            dst_ref=back.at[pl.ds((me * groups + group) * piece, piece)],
            send_sem=bs_sem.at[group, step],
            recv_sem=br_sem.at[group, step],
            device_id={"vel": target},
            device_id_type=MESH,
        )

    def own_in(group):
        return pltpu.make_async_copy(
            sent.at[pl.ds((me * groups + group) * piece, piece)], got.at[group, me],
            own_sem.at[0, group],
        )

    def own_out(group):
        return pltpu.make_async_copy(
            result.at[group, me], back.at[pl.ds((me * groups + group) * piece, piece)],
            own_sem.at[1, group],
        )

    def send(group):
        for step in range(1, n_vel):
            forward(group, step).start()
        own_in(group).start()

    inner = [group for group in range(groups) if 0 < group < groups - 1]
    outer = [group for group in range(groups) if group not in inner]
    if inner:
        for step in [*range(1, n_vel), 0]:
            target = lax.rem(me + step, n_vel)
            first = pl.multiple_of(target * own, SUB)

            @pl.loop(0, rows)
            def _(k):
                lanes = pl.ds(pl.multiple_of(k * LANES, LANES), LANES)
                value = swept(padded[pl.ds(SUB + first, own), lanes], k)
                for tile in range(own // SUB):
                    sent[pl.ds((first + tile * SUB) * rows + k, SUB, stride=rows), :] = value[
                        tile * SUB:(tile + 1) * SUB
                    ]

            for group in inner:
                if step:
                    forward(group, step).start()
                else:
                    own_in(group).start()
    for copy in halo_copies:
        copy.wait()

    total = cells + 2 * SUB
    position = lax.broadcasted_iota(jnp.int32, (total, LANES), 0) + (spot * cells - SUB)
    inside = (position >= 0) & (position < n_space * cells)

    @pl.loop(0, rows)
    def _(k):
        lanes = pl.ds(pl.multiple_of(k * LANES, LANES), LANES)
        padded[SUB - 2:SUB, lanes] = halo_in[0, pl.ds(2 * k, 2), :]
        padded[SUB + cells:SUB + cells + 2, lanes] = halo_in[1, pl.ds(2 * k, 2), :]
        value = swept(jnp.where(inside, padded[:, lanes], 0.0), k, inside)
        for target in range(n_vel):
            for group in outer:
                cell = target * own + group * GROUP
                sent[pl.ds(cell * rows + k, GROUP, stride=rows), :] = value[
                    SUB + cell:SUB + cell + GROUP
                ]

    for group in outer:
        send(group)

    slot = lax.broadcasted_iota(jnp.int32, (cells, cells), 1)
    cell_id = lax.broadcasted_iota(jnp.int32, (cells, cells), 0)
    chosen = slot < BLOCK_CELLS * jnp.broadcast_to(blocks_ref[...], (cells, cells))
    hit = (jnp.broadcast_to(order_ref[...], (cells, cells)) == cell_id) & chosen
    flags = jnp.max(jnp.where(hit, 1.0, 0.0), axis=1, keepdims=True)
    listed_ref[...] = jnp.broadcast_to(flags, (cells, LANES))

    load_raw.wait()
    for copy in load_tables:
        copy.wait()
    for i in range(4):
        high, low = halves(step_ref[i])
        left_ref[i] = jnp.concatenate([high, low, high], axis=1)
    for i in range(2):
        high, low = halves(step_ref[4 + i])
        right_ref[i] = jnp.concatenate([high, high, low], axis=0)
    for k in range(NV * SUB):
        natural[pl.ds(k, KERN, stride=NV * SUB), :] = raw[:, k * LANES:(k + 1) * LANES]
    lane_block = lax.broadcasted_iota(jnp.int32, (SUB, LANES), 1) // NV
    row_r = lax.broadcasted_iota(jnp.int32, (NV * SUB, LANES), 0) // 16 % 8

    @pl.loop(0, KERN)
    def _(table):
        base = table * (NV * SUB)
        for h in range(2):
            for r in range(8):
                for p in (0, 8):
                    packed = None
                    for s in range(4):
                        start = (2 * p + h) * SUB + 2 * s + r // 4
                        block = natural[pl.ds(base + start, SUB, stride=2 * SUB), :]
                        shift = (s - r % 4) % 4 * NV
                        if shift:
                            block = pltpu.roll(block, shift, 1)
                        packed = block if s == 0 else jnp.where(lane_block == s, block, packed)
                    top = h * LANES + r * 16 + p
                    staged[top:top + SUB, :] = packed
        value = staged[...]
        high, low = halves(value)
        lane_moves, row_moves = mirror_ref[:LANES].astype(BF16), mirror_ref[LANES:].astype(BF16)
        moved = jnp.dot(high, lane_moves, preferred_element_type=F32) + jnp.dot(
            low, lane_moves, preferred_element_type=F32
        )
        moved = jnp.where(row_r == 0, moved[:, :LANES], moved[:, LANES:])
        high, low = halves(moved)
        moved = jnp.dot(
            row_moves, jnp.concatenate([high, low], axis=1), preferred_element_type=F32
        )
        moved = moved[:, :LANES] + moved[:, LANES:]
        weight_ref[table] = (value + moved) * (0.5 / NV**3)

    half = NV * SUB // 2

    def work(group):
        def cell(j):
            return jnp.concatenate(
                [got[group, m, j * rows:(j + 1) * rows, :] for m in range(n_vel)], axis=0
            )

        def stacked(lower):
            cut = slice(0, half) if lower else slice(half, 2 * half)
            return jnp.concatenate(
                [
                    jnp.concatenate([cell(2 * i)[cut], cell(2 * i + 1)[cut]], axis=0)
                    for i in range(pairs)
                ],
                axis=1,
            )

        twist_re, twist_im = tw_ref[0], tw_ref[1]
        low, high = stacked(True), stacked(False)
        for h, mixed in enumerate((low + high, low - high)):
            turned = left_dot(left_ref[h], mixed)
            for i in range(pairs):
                re = turned[:half, i * LANES:(i + 1) * LANES]
                im = turned[half:, i * LANES:(i + 1) * LANES]
                spectrum[(2 * i + h) * half:(2 * i + h + 1) * half, :] = jnp.concatenate(
                    [re * twist_re - im * twist_im, re * twist_im + im * twist_re], axis=1
                )
        spectrum[...] = right_dot(spectrum[...], right_ref[0])

        for table in range(KERN):
            weight = weight_ref[table]
            weights = jnp.concatenate([weight] * pairs, axis=0)
            weights = jnp.concatenate([weights, weights], axis=1)
            lined = right_dot(spectrum[...] * weights, right_ref[1])
            halves_out = []
            for h in range(2):
                columns = []
                for i in range(pairs):
                    block = lined[(2 * i + h) * half:(2 * i + h + 1) * half]
                    re, im = block[:, :LANES], block[:, LANES:]
                    columns.append(
                        jnp.concatenate(
                            [re * twist_re + im * twist_im, im * twist_re - re * twist_im], axis=0
                        )
                    )
                halves_out.append(left_dot(left_ref[2 + h], jnp.concatenate(columns, axis=1)))
            even, odd = halves_out
            for place, value in ((0, even + odd), (1, even - odd)):
                if table == 0:
                    parts[place] = value
                elif table == 1:
                    parts[place] = parts[place] * value
                elif table == 2:
                    parts[2 + place] = value
                elif table == 3:
                    parts[place] = parts[place] + parts[2 + place] * value
                else:
                    parts[place] = parts[place] - stacked(place == 0) * value

        for j in range(GROUP):
            flag = listed_ref[pl.ds((me * groups + group) * GROUP + j, 1), :] > 0.0
            i, component = j // 2, j % 2
            for m in range(n_vel):
                place, start = (m * rows) // half, (m * rows) % half
                change = parts[
                    place,
                    component * half + start:component * half + start + rows,
                    i * LANES:(i + 1) * LANES,
                ]
                old = got[group, m, j * rows:(j + 1) * rows, :]
                result[group, m, j * rows:(j + 1) * rows, :] = jnp.where(
                    flag, old + STEP_SCALE * change, old
                )

    def give(group):
        for step in range(1, n_vel):
            backward(group, step).start()
        own_out(group).start()

    turns = inner + outer
    count = len(inner)

    def group_of(turn):
        if groups == 1:
            return turn
        return jnp.where(turn < count, turn + 1, (turn - count) * (groups - 1))

    @pl.loop(0, groups)
    def _(turn):
        group = group_of(turn)
        for step in range(1, n_vel):
            forward(group, step).wait_recv()
        own_in(group).wait()
        if groups > 2:
            @pl.when(turn == groups - 1)
            def _():
                give(group_of(turn - 1))

        work(group)

        if groups > 2:
            @pl.when((turn > 0) & (turn < groups - 1))
            def _():
                give(group_of(turn - 1))

            @pl.when(turn == groups - 1)
            def _():
                give(group)
        else:
            give(group)

    for group in range(groups):
        for step in range(1, n_vel):
            forward(group, step).wait_send()

    def finish(tiles):
        @pl.loop(0, rows)
        def _(k):
            lanes = pl.ds(pl.multiple_of(k * LANES, LANES), LANES)
            for tile in tiles:
                out_ref[tile * SUB:(tile + 1) * SUB, lanes] = back[
                    pl.ds(tile * SUB * rows + k, SUB, stride=rows), :
                ]

    done, ready = set(), set()
    for group in turns:
        for step in range(1, n_vel):
            backward(group, step).wait()
        own_out(group).wait()
        ready.add(group)
        tiles = []
        for tile in range(cells // SUB):
            needs = {cell % own // GROUP for cell in range(tile * SUB, (tile + 1) * SUB)}
            if tile not in done and needs <= ready:
                tiles.append(tile)
        done.update(tiles)
        if tiles:
            finish(tiles)


def local(n_space, n_vel, distribution, collision_order, collision_blocks, kernels):
    cells, width = distribution.shape
    rows = width // LANES
    own = cells // n_vel
    groups = own // GROUP
    piece = GROUP * rows
    constants = [jnp.asarray(c) for c in dft_constants()]
    anywhere = pl.BlockSpec(memory_space=pl.ANY)
    vmem = pl.BlockSpec(memory_space=pltpu.VMEM)
    dma = pltpu.SemaphoreType.DMA
    return pl.pallas_call(
        functools.partial(kernel, n_space, n_vel, cells, width),
        out_shape=jax.ShapeDtypeStruct((cells, width), F32),
        in_specs=[anywhere, vmem, vmem] + [anywhere] * 4,
        out_specs=vmem,
        scratch_shapes=[pltpu.VMEM(c.shape, c.dtype) for c in constants]
        + [
            pltpu.VMEM((cells + 2 * SUB, width), F32),
            pltpu.VMEM((2, 2 * rows, LANES), F32),
            pltpu.VMEM((2, 2 * rows, LANES), F32),
            pltpu.VMEM((cells * rows, LANES), F32),
            pltpu.VMEM((groups, n_vel, piece, LANES), F32),
            pltpu.VMEM((groups, n_vel, piece, LANES), F32),
            pltpu.VMEM((cells * rows, LANES), F32),
            pltpu.VMEM((GROUP // 2 * NV * SUB, 2 * LANES), F32),
            pltpu.VMEM((4, NV * SUB, GROUP // 2 * LANES), F32),
            pltpu.VMEM((4, NV * SUB, 3 * NV * SUB), BF16),
            pltpu.VMEM((2, 3 * NV * SUB, NV * SUB), BF16),
            pltpu.VMEM((KERN, NV**3), F32),
            pltpu.VMEM((KERN * NV * SUB, LANES), F32),
            pltpu.VMEM((KERN, NV * SUB, LANES), F32),
            pltpu.VMEM((NV * SUB, LANES), F32),
            pltpu.VMEM((cells, LANES), F32),
            dma,
            dma,
            dma((len(constants),)),
            dma((2,)),
            dma((2,)),
            dma((groups, n_vel)),
            dma((groups, n_vel)),
            dma((groups, n_vel)),
            dma((groups, n_vel)),
            dma((2, groups)),
        ],
        compiler_params=pltpu.CompilerParams(
            collective_id=0, has_side_effects=True, vmem_limit_bytes=60 * 2**20
        ),
    )(distribution, collision_order, collision_blocks[:, None], kernels, *constants)


def solution(mesh):
    return jax.shard_map(
        functools.partial(local, mesh.shape["space"], mesh.shape["vel"]),
        mesh=mesh,
        in_specs=(P("space", "vel"), P("space", None), P("space"), P()),
        out_specs=P("space", "vel"),
        check_vma=False,
    )
```

```python
import functools
import math

import jax
import jax.numpy as jnp
import numpy as np
from jax import lax
from jax.experimental import pallas as pl
from jax.experimental.pallas import tpu as pltpu
from jax.sharding import PartitionSpec as P

NV = 32
QUAD = 2
BLOCK_CELLS = 16
KERN = 5
STEP_SCALE = 0.25
COURANT_MAX = 0.95
LANES = 128
SUB = 8
GROUP = 4
MESH = pl.DeviceIdType.MESH
F32 = jnp.float32
BF16 = jnp.bfloat16


def left_form(matrix):
    return np.block([[matrix.real, -matrix.imag], [matrix.imag, matrix.real]])


def right_form(matrix):
    return np.block([[matrix.real, matrix.imag], [-matrix.imag, matrix.real]])


def dft_constants():
    turn = lambda phase: np.exp(-2j * math.pi * phase)
    r = np.repeat(np.arange(8), 16)[:, None]
    p = np.tile(np.arange(16), 8)[:, None]
    x0 = np.repeat(np.arange(16), 8)[None, :]
    y1 = np.tile(np.arange(8), 16)[None, :]
    y0 = np.repeat(np.arange(4), 32)[:, None]
    z = np.tile(np.arange(32), 4)[:, None]
    s, qz = y0.T, z.T
    rows = [turn(y1 * r / 8 + x0 * p / 16 + x0 * h / 32) for h in range(2)]
    lanes = turn(y0 * s / 4 + z * qz / 32)
    twist = turn(r * y0.T / 32)
    steps = [left_form(m) for m in rows] + [left_form(m.conj().T) for m in rows]
    steps += [right_form(lanes), right_form(lanes.conj().T)]
    return (
        np.stack(steps).astype(np.float32),
        np.stack([twist.real, twist.imag]).astype(np.float32),
        mirrors().astype(np.float32),
    )


def mirrors():
    lane = np.arange(LANES)
    s, qz = lane // NV, lane % NV
    moves = []
    for carry in range(2):
        source = (-s - carry) % 4 * NV + -qz % NV
        moves.append((lane[:, None] == source[None, :]).astype(np.float64))
    row = np.arange(NV * SUB)
    h, r, p = row // LANES, row // 16 % 8, row % 16
    source = h * LANES + -r % 8 * 16 + (-p - h) % 16
    rows = (source[:, None] == row[None, :]).astype(np.float64)
    return np.concatenate([np.concatenate(moves, axis=1), rows])


def halves(value):
    high = value.astype(BF16)
    return high, (value - high.astype(F32)).astype(BF16)


def left_dot(table, value):
    high, low = halves(value)
    return jnp.dot(table, jnp.concatenate([high, high, low], axis=0), preferred_element_type=F32)


def right_dot(value, table):
    high, low = halves(value)
    return jnp.dot(jnp.concatenate([high, low, high], axis=1), table, preferred_element_type=F32)


def kernel(
    n_space, n_vel, cells, width,
    dist_ref, order_ref, blocks_ref, kernels_ref, *refs,
):
    tables_hbm, out_ref, refs = refs[:3], refs[3], refs[4:]
    tables, refs = refs[:3], refs[3:]
    step_ref, tw_ref, mirror_ref = tables
    (padded, halo_out, halo_in, sent, got, result, back, spectrum, parts,
    left_ref, right_ref, raw, natural, weight_ref, staged, listed_ref, raw_sem, in_sem, table_sem,
    halo_send, halo_recv, fs_sem, fr_sem, bs_sem, br_sem, own_sem) = refs
    rows = width // LANES
    own = cells // n_vel
    groups = own // GROUP
    piece = GROUP * rows
    pairs = GROUP // 2
    me = lax.axis_index("vel")
    spot = lax.axis_index("space")
    right, left = lax.rem(spot + 1, n_space), lax.rem(spot + n_space - 1, n_space)

    load = pltpu.make_async_copy(dist_ref, padded.at[pl.ds(SUB, cells)], in_sem)
    load.start()
    load_raw = pltpu.make_async_copy(kernels_ref, raw, raw_sem)
    load_raw.start()
    load_tables = [
        pltpu.make_async_copy(source, table, table_sem.at[i])
        for i, (source, table) in enumerate(zip(tables_hbm, tables))
    ]
    for copy in load_tables:
        copy.start()
    barrier = pltpu.get_barrier_semaphore()
    for step in range(1, n_vel):
        pl.semaphore_signal(
            barrier, inc=1, device_id={"vel": lax.rem(me + step, n_vel)}, device_id_type=MESH
        )
    for side in (left, right):
        pl.semaphore_signal(barrier, inc=1, device_id={"space": side}, device_id_type=MESH)
    load.wait()

    @pl.loop(0, rows)
    def _(k):
        lanes = pl.ds(pl.multiple_of(k * LANES, LANES), LANES)
        halo_out[0, pl.ds(2 * k, 2), :] = padded[SUB:SUB + 2, lanes]
        halo_out[1, pl.ds(2 * k, 2), :] = padded[SUB + cells - 2:SUB + cells, lanes]

    pl.semaphore_wait(barrier, n_vel + 1)
    halo_copies = []
    for way, side in ((0, left), (1, right)):
        copy = pltpu.make_async_remote_copy(
            src_ref=halo_out.at[way],
            dst_ref=halo_in.at[1 - way],
            send_sem=halo_send.at[way],
            recv_sem=halo_recv.at[1 - way],
            device_id={"space": side},
            device_id_type=MESH,
        )
        copy.start()
        halo_copies.append(copy)

    def swept(value, k, inside=None):
        plane = (me * rows + k) // SUB
        courant = COURANT_MAX * (2.0 * plane.astype(F32) - (NV - 1)) / (NV - 1)
        upwind_pos, upwind_neg = jnp.maximum(courant, 0.0), jnp.minimum(courant, 0.0)
        extent = value.shape[0]
        for _ in range(2):
            before = pltpu.roll(value, 1, 0)
            after = pltpu.roll(value, extent - 1, 0)
            value = value - upwind_pos * (value - before) - upwind_neg * (after - value)
            if inside is not None:
                value = jnp.where(inside, value, 0.0)
        return value

    def forward(group, step):
        target = lax.rem(me + step, n_vel)
        return pltpu.make_async_remote_copy(
            src_ref=sent.at[pl.ds((target * groups + group) * piece, piece)],
            dst_ref=got.at[group, me],
            send_sem=fs_sem.at[group, step],
            recv_sem=fr_sem.at[group, step],
            device_id={"vel": target},
            device_id_type=MESH,
        )

    def backward(group, step):
        target = lax.rem(me + step, n_vel)
        return pltpu.make_async_remote_copy(
            src_ref=result.at[group, target],
            dst_ref=back.at[pl.ds((me * groups + group) * piece, piece)],
            send_sem=bs_sem.at[group, step],
            recv_sem=br_sem.at[group, step],
            device_id={"vel": target},
            device_id_type=MESH,
        )

    def own_in(group):
        return pltpu.make_async_copy(
            sent.at[pl.ds((me * groups + group) * piece, piece)], got.at[group, me],
            own_sem.at[0, group],
        )

    def own_out(group):
        return pltpu.make_async_copy(
            result.at[group, me], back.at[pl.ds((me * groups + group) * piece, piece)],
            own_sem.at[1, group],
        )

    def send(group):
        for step in range(1, n_vel):
            forward(group, step).start()
        own_in(group).start()

    inner = [group for group in range(groups) if 0 < group < groups - 1]
    outer = [group for group in range(groups) if group not in inner]
    if inner:
        for step in [*range(1, n_vel), 0]:
            target = lax.rem(me + step, n_vel)
            first = pl.multiple_of(target * own, SUB)

            @pl.loop(0, rows)
            def _(k):
                lanes = pl.ds(pl.multiple_of(k * LANES, LANES), LANES)
                value = swept(padded[pl.ds(SUB + first, own), lanes], k)
                for tile in range(own // SUB):
                    sent[pl.ds((first + tile * SUB) * rows + k, SUB, stride=rows), :] = value[
                        tile * SUB:(tile + 1) * SUB
                    ]

            for group in inner:
                if step:
                    forward(group, step).start()
                else:
                    own_in(group).start()
    for copy in halo_copies:
        copy.wait()

    total = cells + 2 * SUB
    position = lax.broadcasted_iota(jnp.int32, (total, LANES), 0) + (spot * cells - SUB)
    inside = (position >= 0) & (position < n_space * cells)

    @pl.loop(0, rows)
    def _(k):
        lanes = pl.ds(pl.multiple_of(k * LANES, LANES), LANES)
        padded[SUB - 2:SUB, lanes] = halo_in[0, pl.ds(2 * k, 2), :]
        padded[SUB + cells:SUB + cells + 2, lanes] = halo_in[1, pl.ds(2 * k, 2), :]
        value = swept(jnp.where(inside, padded[:, lanes], 0.0), k, inside)
        for target in range(n_vel):
            for group in outer:
                cell = target * own + group * GROUP
                sent[pl.ds(cell * rows + k, GROUP, stride=rows), :] = value[
                    SUB + cell:SUB + cell + GROUP
                ]

    for group in outer:
        send(group)

    slot = lax.broadcasted_iota(jnp.int32, (cells, cells), 1)
    cell_id = lax.broadcasted_iota(jnp.int32, (cells, cells), 0)
    chosen = slot < BLOCK_CELLS * jnp.broadcast_to(blocks_ref[...], (cells, cells))
    hit = (jnp.broadcast_to(order_ref[...], (cells, cells)) == cell_id) & chosen
    flags = jnp.max(jnp.where(hit, 1.0, 0.0), axis=1, keepdims=True)
    listed_ref[...] = jnp.broadcast_to(flags, (cells, LANES))

    load_raw.wait()
    for copy in load_tables:
        copy.wait()
    for i in range(4):
        high, low = halves(step_ref[i])
        left_ref[i] = jnp.concatenate([high, low, high], axis=1)
    for i in range(2):
        high, low = halves(step_ref[4 + i])
        right_ref[i] = jnp.concatenate([high, high, low], axis=0)
    for k in range(NV * SUB):
        natural[pl.ds(k, KERN, stride=NV * SUB), :] = raw[:, k * LANES:(k + 1) * LANES]
    lane_block = lax.broadcasted_iota(jnp.int32, (SUB, LANES), 1) // NV
    row_r = lax.broadcasted_iota(jnp.int32, (NV * SUB, LANES), 0) // 16 % 8

    @pl.loop(0, KERN)
    def _(table):
        base = table * (NV * SUB)
        for h in range(2):
            for r in range(8):
                for p in (0, 8):
                    packed = None
                    for s in range(4):
                        start = (2 * p + h) * SUB + 2 * s + r // 4
                        block = natural[pl.ds(base + start, SUB, stride=2 * SUB), :]
                        shift = (s - r % 4) % 4 * NV
                        if shift:
                            block = pltpu.roll(block, shift, 1)
                        packed = block if s == 0 else jnp.where(lane_block == s, block, packed)
                    top = h * LANES + r * 16 + p
                    staged[top:top + SUB, :] = packed
        value = staged[...]
        high, low = halves(value)
        lane_moves, row_moves = mirror_ref[:LANES].astype(BF16), mirror_ref[LANES:].astype(BF16)
        moved = jnp.dot(high, lane_moves, preferred_element_type=F32) + jnp.dot(
            low, lane_moves, preferred_element_type=F32
        )
        moved = jnp.where(row_r == 0, moved[:, :LANES], moved[:, LANES:])
        high, low = halves(moved)
        moved = jnp.dot(
            row_moves, jnp.concatenate([high, low], axis=1), preferred_element_type=F32
        )
        moved = moved[:, :LANES] + moved[:, LANES:]
        weight_ref[table] = (value + moved) * (0.5 / NV**3)

    half = NV * SUB // 2

    def work(group):
        def cell(j):
            return jnp.concatenate(
                [got[group, m, j * rows:(j + 1) * rows, :] for m in range(n_vel)], axis=0
            )

        def stacked(lower):
            cut = slice(0, half) if lower else slice(half, 2 * half)
            return jnp.concatenate(
                [
                    jnp.concatenate([cell(2 * i)[cut], cell(2 * i + 1)[cut]], axis=0)
                    for i in range(pairs)
                ],
                axis=1,
            )

        twist_re, twist_im = tw_ref[0], tw_ref[1]
        low, high = stacked(True), stacked(False)
        for h, mixed in enumerate((low + high, low - high)):
            turned = left_dot(left_ref[h], mixed)
            for i in range(pairs):
                re = turned[:half, i * LANES:(i + 1) * LANES]
                im = turned[half:, i * LANES:(i + 1) * LANES]
                spectrum[(2 * i + h) * half:(2 * i + h + 1) * half, :] = jnp.concatenate(
                    [re * twist_re - im * twist_im, re * twist_im + im * twist_re], axis=1
                )
        spectrum[...] = right_dot(spectrum[...], right_ref[0])

        for table in range(KERN):
            weight = weight_ref[table]
            weights = jnp.concatenate([weight] * pairs, axis=0)
            weights = jnp.concatenate([weights, weights], axis=1)
            lined = right_dot(spectrum[...] * weights, right_ref[1])
            halves_out = []
            for h in range(2):
                columns = []
                for i in range(pairs):
                    block = lined[(2 * i + h) * half:(2 * i + h + 1) * half]
                    re, im = block[:, :LANES], block[:, LANES:]
                    columns.append(
                        jnp.concatenate(
                            [re * twist_re + im * twist_im, im * twist_re - re * twist_im], axis=0
                        )
                    )
                halves_out.append(left_dot(left_ref[2 + h], jnp.concatenate(columns, axis=1)))
            even, odd = halves_out
            for place, value in ((0, even + odd), (1, even - odd)):
                if table == 0:
                    parts[place] = value
                elif table == 1:
                    parts[place] = parts[place] * value
                elif table == 2:
                    parts[2 + place] = value
                elif table == 3:
                    parts[place] = parts[place] + parts[2 + place] * value
                else:
                    parts[place] = parts[place] - stacked(place == 0) * value

        for j in range(GROUP):
            flag = listed_ref[pl.ds((me * groups + group) * GROUP + j, 1), :] > 0.0
            i, component = j // 2, j % 2
            for m in range(n_vel):
                place, start = (m * rows) // half, (m * rows) % half
                change = parts[
                    place,
                    component * half + start:component * half + start + rows,
                    i * LANES:(i + 1) * LANES,
                ]
                old = got[group, m, j * rows:(j + 1) * rows, :]
                result[group, m, j * rows:(j + 1) * rows, :] = jnp.where(
                    flag, old + STEP_SCALE * change, old
                )

    def give(group):
        for step in range(1, n_vel):
            backward(group, step).start()
        own_out(group).start()

    turns = inner + outer
    count = len(inner)

    def group_of(turn):
        if groups == 1:
            return turn
        return jnp.where(turn < count, turn + 1, (turn - count) * (groups - 1))

    @pl.loop(0, groups)
    def _(turn):
        group = group_of(turn)
        for step in range(1, n_vel):
            forward(group, step).wait_recv()
        own_in(group).wait()
        work(group)
        give(group)

    for group in range(groups):
        for step in range(1, n_vel):
            forward(group, step).wait_send()

    for group in turns:
        for step in range(1, n_vel):
            backward(group, step).wait()
        own_out(group).wait()
        for source in range(n_vel):
            part = pl.ds((source * groups + group) * piece, piece)
            out_ref[part, :] = back[part, :]


def regrid(rows, in_ref, out_ref):
    for k in range(rows):
        out_ref[:, k * LANES:(k + 1) * LANES] = in_ref[pl.ds(k, SUB, stride=rows), :]


def local(n_space, n_vel, distribution, collision_order, collision_blocks, kernels):
    cells, width = distribution.shape
    rows = width // LANES
    own = cells // n_vel
    groups = own // GROUP
    piece = GROUP * rows
    constants = [jnp.asarray(c) for c in dft_constants()]
    anywhere = pl.BlockSpec(memory_space=pl.ANY)
    vmem = pl.BlockSpec(memory_space=pltpu.VMEM)
    dma = pltpu.SemaphoreType.DMA
    moved = pl.pallas_call(
        functools.partial(kernel, n_space, n_vel, cells, width),
        out_shape=jax.ShapeDtypeStruct((cells * rows, LANES), F32),
        in_specs=[anywhere, vmem, vmem] + [anywhere] * 4,
        out_specs=vmem,
        scratch_shapes=[pltpu.VMEM(c.shape, c.dtype) for c in constants]
        + [
            pltpu.VMEM((cells + 2 * SUB, width), F32),
            pltpu.VMEM((2, 2 * rows, LANES), F32),
            pltpu.VMEM((2, 2 * rows, LANES), F32),
            pltpu.VMEM((cells * rows, LANES), F32),
            pltpu.VMEM((groups, n_vel, piece, LANES), F32),
            pltpu.VMEM((groups, n_vel, piece, LANES), F32),
            pltpu.VMEM((cells * rows, LANES), F32),
            pltpu.VMEM((GROUP // 2 * NV * SUB, 2 * LANES), F32),
            pltpu.VMEM((4, NV * SUB, GROUP // 2 * LANES), F32),
            pltpu.VMEM((4, NV * SUB, 3 * NV * SUB), BF16),
            pltpu.VMEM((2, 3 * NV * SUB, NV * SUB), BF16),
            pltpu.VMEM((KERN, NV**3), F32),
            pltpu.VMEM((KERN * NV * SUB, LANES), F32),
            pltpu.VMEM((KERN, NV * SUB, LANES), F32),
            pltpu.VMEM((NV * SUB, LANES), F32),
            pltpu.VMEM((cells, LANES), F32),
            dma,
            dma,
            dma((len(constants),)),
            dma((2,)),
            dma((2,)),
            dma((groups, n_vel)),
            dma((groups, n_vel)),
            dma((groups, n_vel)),
            dma((groups, n_vel)),
            dma((2, groups)),
        ],
        compiler_params=pltpu.CompilerParams(
            collective_id=0, has_side_effects=True, vmem_limit_bytes=60 * 2**20
        ),
    )(distribution, collision_order, collision_blocks[:, None], kernels, *constants)
    return pl.pallas_call(
        functools.partial(regrid, rows),
        grid=(cells // SUB,),
        out_shape=jax.ShapeDtypeStruct((cells, width), F32),
        in_specs=[pl.BlockSpec((SUB * rows, LANES), lambda i: (i, 0))],
        out_specs=pl.BlockSpec((SUB, width), lambda i: (i, 0)),
        compiler_params=pltpu.CompilerParams(vmem_limit_bytes=60 * 2**20),
    )(moved)


def solution(mesh):
    return jax.shard_map(
        functools.partial(local, mesh.shape["space"], mesh.shape["vel"]),
        mesh=mesh,
        in_specs=(P("space", "vel"), P("space", None), P("space"), P()),
        out_specs=P("space", "vel"),
        check_vma=False,
    )
```
